32 devices in a mesh: sub: 8 (over z, y), mode: 4 (over x, core).
Axes of the slice: x: 2, y: 2, z: 4, core: 2. Of those that a mesh axis runs over, the one named last changes fastest.
Arguments:
- panels: bfloat16 [8, 2048, 768], P('sub', 'mode'), may hold values from -0.59765625 to 0.59765625
- eigvals: float32 [8, 2048], P('sub', 'mode'), may hold values from 0.5 to 20
- counts: int32 [8], P('sub'), may hold values from 512 to 2048, as said below
- separator_diag: float32 [8, 768], P('sub'), may hold values from 4 to 8
- separator_index_tables: int32 [8, 768], replicated, may hold values from 0 to 767, each once within a row
Outputs:
- condensed: float32 [768, 768], P('sub')
The draws below stay inside these ranges and needn't reach their ends.
Inputs may be any that keep to these rules, and one draw needn't show every extreme that they name: `counts`: every value from 512 to 2048 can occur, and both ends occur in every draw. `separator_index_tables`: each row is a permutation of 0 to 767.
All inputs are finite; a program needn't handle non-finite values.
Results may differ from the reference program's by a relative error of at most 0.0003.
Values sent between devices are 32-bit elements; how exact they have to be, the bound alone decides.
A program may use at most 64 MiB of HBM per device.

```python
import math
import jax
import jax.numpy as jnp
from jax import lax

SEP = 768
MODES = 2048
NSUB = 8


def draw_counts(key, part):
    key_base, key_high, key_low = jax.random.split(key, 3)
    values = jax.random.randint(key_base, (NSUB,), MODES // 4, MODES + 1, dtype=jnp.int32)
    high_pos = jax.random.randint(key_high, (), 0, NSUB, dtype=jnp.int32)
    low_pos = (high_pos + 1 + jax.random.randint(key_low, (), 0, NSUB - 1, dtype=jnp.int32)) % NSUB
    values = values.at[high_pos].set(MODES)
    values = values.at[low_pos].set(MODES // 4)
    return values


def block_scale(key, extent, pieces, least, high):
    def one(axis_at, shards_of):
        heights = jax.random.uniform(jax.random.fold_in(jax.random.fold_in(key, 6), axis_at), (shards_of,), jnp.float32, least / len(pieces), high / len(pieces))
        return jnp.repeat(jnp.exp(heights), extent[axis_at] // shards_of).reshape((-1,) + (1,) * (len(extent) - axis_at - 1))

    loudness = one(*pieces[0])
    for cut in pieces[1:]:
        loudness = loudness * one(*cut)
    return loudness


def bell_draw(key, dims, deviation, most, pieces=(), kind=jnp.bfloat16):
    level = block_scale(key, dims, pieces, -0.22, 0.18) if pieces else 1.0
    result = jax.random.normal(key, dims, jnp.float32) * deviation * level
    return jnp.minimum(jnp.maximum(result, -most), most).astype(kind)


def setup_inputs(seed: int = 0) -> dict:
    arg_keys = jax.random.split(jax.random.key(seed), 6)
    panels = bell_draw(arg_keys[0], (NSUB, MODES, SEP), 0.1, 0.59765625, ((0, 8), (1, 4)))
    eigvals = jnp.clip(jnp.exp(math.log(20.0) - 3.6888795 * jax.random.uniform(arg_keys[1], (NSUB, MODES), jnp.float32) ** block_scale(arg_keys[1], (NSUB, MODES), ((0, 8), (1, 4)), -0.2, 0.2)), 0.5, 20.0)
    counts = draw_counts(jax.random.fold_in(arg_keys[5], 71), 0)
    separator_diag = jnp.clip(4.0 + 4.0 * jax.random.uniform(arg_keys[3], (NSUB, SEP), jnp.float32) ** block_scale(arg_keys[3], (NSUB, SEP), ((0, 8),), -0.2, 0.2), 4.0, 8.0)
    separator_index_tables = jax.vmap(lambda own: jax.random.permutation(own, SEP))(jax.random.split(arg_keys[4], NSUB)).reshape((NSUB, SEP)).astype(jnp.int32)
    return dict(panels=panels, eigvals=eigvals, counts=counts, separator_diag=separator_diag, separator_index_tables=separator_index_tables)


def node_perm(separator_index_tables, level_number, nodes):
    span_rows = 2 ** level_number
    map_rows = nodes * span_rows + span_rows - 1
    shifted = (jnp.arange(SEP, dtype=jnp.int32) + 97 * level_number % SEP) % SEP
    return separator_index_tables[map_rows][:, shifted]

def relabel_equations(schur_remainder_patch, arrangement_list):
    rows_first = jnp.take(schur_remainder_patch, arrangement_list, axis=0)
    return jnp.take(rows_first.T, arrangement_list, axis=0).T

def leaf_tile(operands):
    panel_rows, eig_row, live_count, diag_row = operands
    live_mask = (jnp.arange(MODES, dtype=jnp.int32) < live_count).astype(jnp.float32)
    weighted = (panel_rows.astype(jnp.float32) * (live_mask / eig_row)[:, None]).astype(jnp.bfloat16)
    partial_sum = jnp.dot(weighted.T, panel_rows, preferred_element_type=jnp.float32)
    return jnp.diag(diag_row) - partial_sum

def reference(panels, eigvals, counts, separator_diag, separator_index_tables):
    piled_patches = lax.map(leaf_tile, (panels, eigvals, counts, separator_diag))
    levels_total = NSUB.bit_length() - 1
    for level_number in range(levels_total):
        count_now = piled_patches.shape[0]
        reorder_layers = node_perm(separator_index_tables, level_number, jnp.arange(count_now, dtype=jnp.int32))
        reordered_submatrix = jax.vmap(relabel_equations)(piled_patches, reorder_layers)
        piled_patches = reordered_submatrix[0::2] + reordered_submatrix[1::2]
    return piled_patches[0] * (1.0 / math.sqrt(NSUB))
```

```python
import functools
import math

import jax
import jax.numpy as jnp
from jax import lax
from jax.experimental import pallas as pl
from jax.experimental.pallas import tpu as pltpu
from jax.sharding import PartitionSpec as P

MESH = pl.DeviceIdType.MESH
NT = (((1,), (1,)), ((), ()))
LANES = 128


def plan(subs, modes):
    if subs == 8 and modes == 4:
        x, y, near, far = ("mode", 1), ("sub", 0), ("sub", 1), ("sub", 2)
        return [
            [(True, *x), (True, *y), (True, *near), (True, *far)],
            [(True, *y), (True, *near), (True, *far), (False, *x)],
            [(True, *near), (True, *x), (True, *y), (True, *far)],
        ], 2, 2
    sub_bits, mode_bits = subs.bit_length() - 1, modes.bit_length() - 1
    steps = [(True, "sub", b) for b in range(sub_bits)]
    steps += [(False, "mode", b) for b in range(1, mode_bits)]
    return [steps] * 3, 1, 1


def bit_of(value, bit):
    return (value // 2**bit) % 2


def body(subs, modes, column_parts, pieces, shares, *refs):
    panels_hbm, eig_hbm, counts_ref, diag_hbm, tables_hbm, out_ref = refs[:6]
    panels_ref, eig_ref, diag_ref, tables_ref, load_sems = refs[-5:]
    wt, pt, to_core, from_core, fin, core_sems, fin_sems, send_sems, recv_sems = refs[6:15]
    parts = [part for part in column_parts for _ in range(shares)]
    order = [q * shares + h for h in range(shares) for q in range(len(column_parts))]
    steps = len(parts[0])
    accs = refs[15 : 15 + steps + 1]
    lands = refs[15 + steps + 1 : -5]
    count, chunks = len(parts), len(column_parts)
    loads = [
        pltpu.make_async_copy(source, kept, load_sems.at[i])
        for i, (source, kept) in enumerate(
            [
                (tables_hbm, tables_ref),
                (panels_hbm, panels_ref),
                (eig_hbm, eig_ref),
                (diag_hbm, diag_ref),
            ]
        )
    ]
    for load in loads:
        load.start()
    sub_me, mode_me = lax.axis_index("sub"), lax.axis_index("mode")
    core_me = mode_me % 2
    sep = panels_ref.shape[1]
    depth = panels_ref.shape[0]
    rows = sep // subs // pieces // shares
    place = {"sub": sub_me, "mode": mode_me}

    def partner(axis, bit):
        here = place[axis]
        other = here + 2**bit * (1 - 2 * bit_of(here, bit))
        return (other, mode_me) if axis == "sub" else (sub_me, other)

    sibling = partner("mode", 0)
    links = sorted({step[1:] for part in parts for step in part} | {("mode", 0)})
    barrier = pltpu.get_barrier_semaphore()
    for axis, bit in links:
        pl.semaphore_signal(barrier, inc=1, device_id=partner(axis, bit), device_id_type=MESH)

    first = lax.broadcasted_iota(jnp.int32, (sep, 1), 0)
    across = (sub_me, partner("mode", 1)[1] + 1 - 2 * core_me) if pieces == 2 else None
    greeted = len(links) + (pieces == 2)
    if pieces == 2:
        pl.semaphore_signal(barrier, inc=1, device_id=across, device_id_type=MESH)

    runs = sep // LANES
    place_in_run = lax.broadcasted_iota(jnp.int32, (LANES, sep), 0)
    run_row = lax.broadcasted_iota(jnp.int32, (8, sep), 0)
    run_of = lax.broadcasted_iota(jnp.int32, (8, LANES), 0)
    loads[0].wait()
    index = lax.broadcasted_iota(jnp.int32, (1, sep), 1)
    for level in reversed(range(subs.bit_length() - 1)):
        index = index + 97 * level % sep
        index = jnp.where(index >= sep, index - sep, index)
        line = (sub_me // 2**level) * 2**level + 2**level - 1
        row = tables_ref[pl.ds(line, 1), :]
        table = jnp.zeros((8, LANES), jnp.int32)
        for run in range(runs):
            table = jnp.where(run_of == run, row[:, run * LANES : (run + 1) * LANES], table)
        digits = jnp.concatenate([table // 16, table % 16], axis=0).astype(jnp.float32).astype(jnp.bfloat16)
        mark = jnp.where(place_in_run == index % LANES, 1.0, 0.0).astype(jnp.bfloat16)
        found = jnp.dot(digits, mark, preferred_element_type=jnp.float32)
        value = jnp.where(run_row == index // LANES, found[0:8] * 16.0 + found[8:16], 0.0)
        index = jnp.sum(value, axis=0, keepdims=True).astype(jnp.int32)
    target = jnp.broadcast_to(index, (8, sep)).T[:, 0:1]
    lanes = lax.broadcasted_iota(jnp.int32, (sep, sep), 1)
    moved = jnp.where(target == lanes, 1.0, 0.0).astype(jnp.bfloat16)

    for load in loads[1:]:
        load.wait()
    live = lax.broadcasted_iota(jnp.int32, (1, depth), 1) + mode_me * depth < counts_ref[0]
    scale = jnp.where(live, 1.0, 0.0) / eig_ref[...]
    panels_t = lax.dot_general(moved, panels_ref[...], NT, preferred_element_type=jnp.float32)
    pt[...] = panels_t.astype(jnp.bfloat16)
    wt[...] = (panels_t * scale).astype(jnp.bfloat16)

    diag = diag_ref[...] * jnp.where(mode_me == 0, 1.0, 0.0)
    top = diag.astype(jnp.bfloat16).astype(jnp.float32)
    middle = (diag - top).astype(jnp.bfloat16).astype(jnp.float32)
    low = diag - top - middle
    pick = lax.broadcasted_iota(jnp.int32, (16, sep), 0)
    split = jnp.where(pick == 0, top, jnp.where(pick == 1, middle, jnp.where(pick == 2, low, 0.0)))
    got = lax.dot_general(moved, split.astype(jnp.bfloat16), NT, preferred_element_type=jnp.float32)
    diag_moved = got[:, 0:1] + got[:, 1:2] + got[:, 2:3]
    columns = lax.broadcasted_iota(jnp.int32, (sep, LANES), 1)

    def tile(core, p):
        start = pl.multiple_of((core * chunks + p) * LANES, LANES)
        product = lax.dot_general(
            wt[...], pt[pl.ds(start, LANES), :], NT, preferred_element_type=jnp.float32
        )
        on_diag = columns + start == first
        return jnp.where(on_diag, diag_moved, 0.0) - product

    def slot_of(p, block):
        slot, taken = 0, 0
        for halve, axis, bit in parts[p]:
            if halve:
                if axis == "sub":
                    far = (bit_of(block // pieces, bit) + bit_of(sub_me, bit)) % 2
                else:
                    far = (bit_of(block % pieces, bit - 1) + bit_of(mode_me, bit)) % 2
                    taken = 1
                slot = slot * 2 + far
        return slot if taken else slot * pieces + block % pieces

    def core_copy(p):
        return pltpu.make_async_remote_copy(
            to_core.at[p], from_core.at[p], core_sems.at[0, p], core_sems.at[1, p], sibling, MESH
        )

    blocks = subs * pieces
    def store_tile(kept, core, chunk):
        value = tile(core, chunk)
        for b in range(blocks):
            slot = slot_of(chunk * shares, b)
            for h in range(shares):
                at = (b * shares + h) * rows
                kept[chunk * shares + h, slot, :, :] = value[at : at + rows]

    for chunk in range(chunks):
        store_tile(to_core, 1 - core_me, chunk)
        if chunk == 0:
            pl.semaphore_wait(barrier, greeted)
        for h in range(shares):
            core_copy(chunk * shares + h).start()

    sizes = []
    for p in range(count):
        n, own = blocks, []
        for halve, _, _ in parts[p]:
            n = n // 2 if halve else n
            own.append(n)
        sizes.append(own)

    def exchange(p, k):
        halve, axis, bit = parts[p][k]
        n = sizes[p][k]
        return pltpu.make_async_remote_copy(
            accs[k].at[p, pl.ds(n if halve else 0, n)],
            lands[k].at[p, pl.ds(0, n)],
            send_sems.at[p, k],
            recv_sems.at[p, k],
            partner(axis, bit),
            MESH,
        )

    for chunk in range(chunks):
        store_tile(accs[0], core_me, chunk)
    for p in order:
        core_copy(p).wait_recv()
        accs[0][p] = accs[0][p] + from_core[p]
        exchange(p, 0).start()

    cut = [any(halve and axis == "mode" for halve, axis, _ in part) for part in parts]
    piece_me = bit_of(mode_me, 1)

    def last_copies(p):
        spot = fin.at[core_me, p, pl.ds(piece_me, 1)] if cut[p] else fin.at[core_me, p]
        targets = [sibling, partner("mode", 1), across] if cut[p] else [sibling]
        return [
            pltpu.make_async_remote_copy(spot, spot, fin_sems.at[0, p, i], fin_sems.at[1, p, i], target, MESH)
            for i, target in enumerate(targets)
        ]

    for k in range(steps):
        for p in order:
            n = sizes[p][k]
            exchange(p, k).wait_recv()
            total = accs[k][p, 0:n] + lands[k][p, 0:n]
            if k < steps - 1:
                accs[k + 1][p, 0:n] = total
                exchange(p, k + 1).start()
                continue
            if cut[p]:
                fin[core_me, p, pl.ds(piece_me, 1)] = total
            else:
                fin[core_me, p] = total
            for copy in last_copies(p):
                copy.start()
    for p in order:
        for copy in last_copies(p):
            copy.wait_recv()
    for c in range(2):
        for p in range(count):
            at = (c * chunks + p // shares) * LANES
            for piece in range(pieces):
                down = (piece * shares + p % shares) * rows
                out_ref[down : down + rows, at : at + LANES] = fin[c, p, piece]
    for p in range(count):
        core_copy(p).wait_send()
        for k in range(steps):
            exchange(p, k).wait_send()
        for copy in last_copies(p):
            copy.wait_send()


def solution(mesh):
    subs, modes = mesh.shape["sub"], mesh.shape["mode"]
    column_parts, pieces, shares = plan(subs, modes)
    parts = [part for part in column_parts for _ in range(shares)]

    def local(panels, eigvals, counts, separator_diag, tables):
        sep, depth = panels.shape[2], panels.shape[1]
        own = sep // subs
        rows = own // pieces // shares
        count, steps, blocks = len(parts), len(parts[0]), subs * pieces
        f32 = jnp.float32

        def room(k):
            most = 0
            for part in parts:
                n = blocks
                for halve, _, _ in part[:k]:
                    n = n // 2 if halve else n
                most = max(most, n)
            return pltpu.VMEM((count, most, rows, LANES), f32)

        dma = pltpu.SemaphoreType.DMA
        root = pl.pallas_call(
            functools.partial(body, subs, modes, column_parts, pieces, shares),
            out_shape=jax.ShapeDtypeStruct((own, sep), f32),
            in_specs=[
                pl.BlockSpec(memory_space=pltpu.HBM),
                pl.BlockSpec(memory_space=pltpu.HBM),
                pl.BlockSpec(memory_space=pltpu.SMEM),
                pl.BlockSpec(memory_space=pltpu.HBM),
                pl.BlockSpec(memory_space=pltpu.HBM),
            ],
            out_specs=pl.BlockSpec(memory_space=pltpu.VMEM),
            scratch_shapes=[
                pltpu.VMEM((sep, depth), jnp.bfloat16),
                pltpu.VMEM((sep, depth), jnp.bfloat16),
                pltpu.VMEM((count, blocks, rows, LANES), f32),
                pltpu.VMEM((count, blocks, rows, LANES), f32),
                pltpu.VMEM((2, count, pieces, rows, LANES), f32),
                dma((2, count)),
                dma((2, count, 3)),
                dma((count, steps)),
                dma((count, steps)),
                *[room(k) for k in range(steps + 1)],
                *[room(k + 1) for k in range(steps)],
                pltpu.VMEM((depth, sep), panels.dtype),
                pltpu.VMEM(eigvals.shape, f32),
                pltpu.VMEM(separator_diag.shape, f32),
                pltpu.VMEM(tables.shape, tables.dtype),
                dma((4,)),
            ],
            compiler_params=pltpu.CompilerParams(
                collective_id=0, has_side_effects=True, vmem_limit_bytes=48 * 2**20
            ),
        )(*[pltpu.with_memory_space_constraint(a, pltpu.HBM) for a in (panels[0], eigvals)], counts, *[pltpu.with_memory_space_constraint(a, pltpu.HBM) for a in (separator_diag, tables)])
        return root * (1.0 / math.sqrt(subs))

    return jax.shard_map(
        local,
        mesh=mesh,
        in_specs=(P("sub", "mode", None), P("sub", "mode"), P("sub"), P("sub", None), P()),
        out_specs=P("sub", None),
        check_vma=False,
    )
```

```python
import functools
import math

import jax
import jax.numpy as jnp
from jax import lax
from jax.experimental import pallas as pl
from jax.experimental.pallas import tpu as pltpu
from jax.sharding import PartitionSpec as P

MESH = pl.DeviceIdType.MESH
NT = (((1,), (1,)), ((), ()))
LANES = 128
CORE = ("mode", 0)
SHARES = 2


def plan(subs, modes):
    if subs == 8 and modes == 4:
        x, y, near, far = ("mode", 1), ("sub", 0), ("sub", 1), ("sub", 2)
        return [
            [("halve", (x,)), ("halve", (y, near)), ("halve", (far,))],
            [("halve", (y,)), ("halve", (x, near)), ("halve", (far,))],
            [("halve", (near,)), ("halve", (x, y)), ("halve", (far,))],
        ], 2, SHARES
    sub_bits, mode_bits = subs.bit_length() - 1, modes.bit_length() - 1
    steps = [("halve", (("sub", b),)) for b in range(sub_bits)]
    steps += [("full", (("mode", b),)) for b in range(1, mode_bits)]
    return [steps] * 3, 1, 1


def halved(phase):
    kind, dims = phase
    return dims if kind == "halve" else ()


def members(dims):
    return [
        (mask, tuple(d for i, d in enumerate(dims) if mask >> (len(dims) - 1 - i) & 1))
        for mask in range(1, 2 ** len(dims))
    ]


def bit_of(value, bit):
    return (value // 2**bit) % 2


def body(subs, modes, column_parts, pieces, shares, *refs):
    panels_hbm, eig_hbm, counts_ref, diag_hbm, tables_hbm, out_ref = refs[:6]
    panels_ref, eig_ref, diag_ref, tables_ref, load_sems = refs[-5:]
    wt, pt, to_core, from_core, fin, core_sems, fin_sems, send_sems, recv_sems = refs[6:15]
    parts = [part for part in column_parts for _ in range(shares)]
    chunks = len(column_parts)
    order = [q * shares + h for h in range(shares) for q in range(chunks)]
    steps = len(parts[0])
    accs = refs[15 : 15 + steps]
    lands = refs[15 + steps : -5]
    count = len(parts)
    loads = [
        pltpu.make_async_copy(source, kept, load_sems.at[i])
        for i, (source, kept) in enumerate(
            [
                (tables_hbm, tables_ref),
                (panels_hbm, panels_ref),
                (eig_hbm, eig_ref),
                (diag_hbm, diag_ref),
            ]
        )
    ]
    for load in loads:
        load.start()
    sub_me, mode_me = lax.axis_index("sub"), lax.axis_index("mode")
    core_me = mode_me % 2
    depth, sep = panels_ref.shape
    rows = sep // subs // pieces // shares
    blocks = subs * pieces
    place = {"sub": sub_me, "mode": mode_me}

    def partner(dims):
        there = dict(place)
        for axis, bit in dims:
            there[axis] = there[axis] + 2**bit * (1 - 2 * bit_of(place[axis], bit))
        return there["sub"], there["mode"]

    gather = [(CORE,)] if pieces == 1 else [(CORE,), (("mode", 1),), (CORE, ("mode", 1))]
    greeted = {tuple(sorted(dims)) for part in parts for _, group in part for _, dims in members(group)}
    greeted = sorted(greeted | set(gather))
    barrier = pltpu.get_barrier_semaphore()
    for dims in greeted:
        pl.semaphore_signal(barrier, inc=1, device_id=partner(dims), device_id_type=MESH)

    runs = sep // LANES
    lane = lax.broadcasted_iota(jnp.int32, (8, LANES), 1)
    run_of = lax.broadcasted_iota(jnp.int32, (8, LANES), 0)

    def look_up(line, at):
        found = jnp.zeros((8, LANES), line.dtype)
        for run in range(runs):
            table = jnp.broadcast_to(line[:, run * LANES : (run + 1) * LANES], (8, LANES))
            here = jnp.take_along_axis(table, at % LANES, axis=1)
            found = jnp.where(at // LANES == run, here, found)
        return found

    loads[0].wait()
    index = run_of * LANES + lane
    for level in reversed(range(subs.bit_length() - 1)):
        index = index + 97 * level % sep
        index = jnp.where(index >= sep, index - sep, index)
        at = (sub_me // 2**level) * 2**level + 2**level - 1
        index = look_up(tables_ref[pl.ds(at, 1), :], index)
    target = jnp.concatenate([index.T[:, run : run + 1] for run in range(runs)], axis=0)
    moved = jnp.where(
        target == lax.broadcasted_iota(jnp.int32, (sep, sep), 1), 1.0, 0.0
    ).astype(jnp.bfloat16)

    for load in loads[1:]:
        load.wait()
    live = lax.broadcasted_iota(jnp.int32, (1, depth), 1) + mode_me * depth < counts_ref[0]
    scale = jnp.where(live, 1.0, 0.0) / eig_ref[...]
    panels_t = lax.dot_general(moved, panels_ref[...], NT, preferred_element_type=jnp.float32)
    pt[...] = panels_t.astype(jnp.bfloat16)
    wt[...] = (panels_t * scale).astype(jnp.bfloat16)
    diag = look_up(diag_ref[...] * jnp.where(mode_me < 2, 1.0, 0.0), index)

    tall = rows * shares
    gathered = tall % 16 == 0
    off_diag = lax.broadcasted_iota(jnp.int32, (tall, LANES), 1) - lax.broadcasted_iota(
        jnp.int32, (tall, LANES), 0
    )

    def block_at(q, slot):
        sub, piece, bit_at = sub_me, bit_of(mode_me, 1) if pieces == 2 else 0, blocks.bit_length() - 2
        for phase in column_parts[q]:
            for axis, bit in halved(phase):
                if slot >> bit_at & 1:
                    if axis == "sub":
                        sub = sub + 2**bit * (1 - 2 * bit_of(sub_me, bit))
                    else:
                        piece = 1 - piece
                bit_at -= 1
        return sub * pieces + piece

    def slot_of(q, block):
        slot = 0
        for phase in column_parts[q]:
            for axis, bit in halved(phase):
                slot = slot * 2 + (block >> bit & 1) + bit_of(sub_me, bit) * (1 - 2 * (block >> bit & 1))
        return slot

    def form(q, slots):
        first = [pl.multiple_of((q * 2 + c) * LANES, LANES) for c in (1 - core_me, core_me)]
        columns = jnp.concatenate([pt[pl.ds(start, LANES), :] for start in first], axis=0)
        if gathered:
            starts = [pl.multiple_of(block_at(q, slot) * tall, 16) for slot in slots]
            left = jnp.concatenate([wt[pl.ds(start, tall), :] for start in starts], axis=0)
        else:
            starts = [block * tall for block in range(blocks)]
            slots = [slot_of(q, block) for block in range(blocks)]
            left = wt[...]
        product = lax.dot_general(left, columns, NT, preferred_element_type=jnp.float32)
        for i, slot in enumerate(slots):
            for h in range(shares):
                at = i * tall + h * rows
                to_core[q * shares + h, slot, :, :] = -product[at : at + rows, 0:LANES]
        mine = jnp.where(core_me == 0, diag[2 * q : 2 * q + 1], diag[2 * q + 1 : 2 * q + 2])
        for i, (slot, start) in enumerate(zip(slots, starts)):
            on_diag = jnp.where(off_diag == start - first[1], mine, 0.0)
            value = on_diag - product[i * tall : (i + 1) * tall, LANES : 2 * LANES]
            for h in range(shares):
                accs[0][q * shares + h, slot, :, :] = value[h * rows : (h + 1) * rows]

    bands = [(blocks // 2, blocks // 2), (0, blocks // 2)] if gathered else [(0, blocks)]

    def core_copy(q, band):
        at, n = bands[band]
        group = pl.ds(q * shares, shares)
        return pltpu.make_async_remote_copy(
            to_core.at[group, pl.ds(at, n)],
            from_core.at[group, pl.ds(at, n)],
            core_sems.at[0, q, band],
            core_sems.at[1, q, band],
            partner((CORE,)),
            MESH,
        )

    sizes = []
    for p in range(count):
        n, own = blocks, []
        for phase in parts[p]:
            n = n >> len(halved(phase))
            own.append(n)
        sizes.append(own)

    def exchange(p, k):
        kind, dims = parts[p][k]
        n = sizes[p][k]
        return [
            pltpu.make_async_remote_copy(
                accs[k].at[p, pl.ds(mask * n if kind == "halve" else 0, n)],
                lands[k].at[p, pl.ds((mask - 1) * n, n)],
                send_sems.at[p, k, mask - 1],
                recv_sems.at[p, k, mask - 1],
                partner(other),
                MESH,
            )
            for mask, other in members(dims)
        ]

    for band, (at, n) in enumerate(bands):
        for q in range(chunks):
            form(q, range(at, at + n))
            if band == 0 and q == 0:
                pl.semaphore_wait(barrier, len(greeted))
            core_copy(q, band).start()
    for band, (at, n) in enumerate(bands):
        for q in range(chunks):
            core_copy(q, band).wait_recv()
            for p in range(q * shares, (q + 1) * shares):
                accs[0][p, at : at + n] = accs[0][p, at : at + n] + from_core[p, at : at + n]
                if band == 0:
                    for copy in exchange(p, 0):
                        copy.start()

    piece_me = bit_of(mode_me, 1)

    def last_copies(p):
        spot = fin.at[core_me, p, pl.ds(piece_me, 1)] if pieces == 2 else fin.at[core_me, p]
        return [
            pltpu.make_async_remote_copy(
                spot, spot, fin_sems.at[0, p, i], fin_sems.at[1, p, i], partner(dims), MESH
            )
            for i, dims in enumerate(gather)
        ]

    for k in range(steps):
        for p in order:
            n = sizes[p][k]
            total = accs[k][p, 0:n]
            for copy in exchange(p, k):
                copy.wait_recv()
            for mask, _ in members(parts[p][k][1]):
                total = total + lands[k][p, (mask - 1) * n : mask * n]
            if k < steps - 1:
                accs[k + 1][p, 0:n] = total
                for copy in exchange(p, k + 1):
                    copy.start()
                continue
            if pieces == 2:
                fin[core_me, p, pl.ds(piece_me, 1)] = total
            else:
                fin[core_me, p] = total
            for copy in last_copies(p):
                copy.start()
    for p in order:
        for copy in last_copies(p):
            copy.wait_recv()
    for c in range(2):
        for p in range(count):
            at = (p // shares * 2 + c) * LANES
            for piece in range(pieces):
                down = (piece * shares + p % shares) * rows
                out_ref[down : down + rows, at : at + LANES] = fin[c, p, piece]
    for q in range(chunks):
        for band in range(len(bands)):
            core_copy(q, band).wait_send()
    for p in range(count):
        for k in range(steps):
            for copy in exchange(p, k):
                copy.wait_send()
        for copy in last_copies(p):
            copy.wait_send()


def solution(mesh):
    subs, modes = mesh.shape["sub"], mesh.shape["mode"]
    column_parts, pieces, shares = plan(subs, modes)
    parts = [part for part in column_parts for _ in range(shares)]

    def local(panels, eigvals, counts, separator_diag, tables):
        sep, depth = panels.shape[2], panels.shape[1]
        own = sep // subs
        rows = own // pieces // shares
        count, steps, blocks = len(parts), len(parts[0]), subs * pieces
        f32 = jnp.float32

        def held(part, k):
            return blocks >> sum(len(halved(phase)) for phase in part[:k])

        def room(k):
            return pltpu.VMEM((count, max(held(part, k) for part in parts), rows, LANES), f32)

        def landing(k):
            most = max((2 ** len(part[k][1]) - 1) * held(part, k + 1) for part in parts)
            return pltpu.VMEM((count, most, rows, LANES), f32)

        most_copies = max(2 ** len(dims) - 1 for part in parts for _, dims in part)
        dma = pltpu.SemaphoreType.DMA
        panels, eigvals, separator_diag, tables = [
            pltpu.with_memory_space_constraint(a, pltpu.HBM)
            for a in (panels[0], eigvals, separator_diag, tables)
        ]
        root = pl.pallas_call(
            functools.partial(body, subs, modes, column_parts, pieces, shares),
            out_shape=jax.ShapeDtypeStruct((own, sep), f32),
            in_specs=[
                pl.BlockSpec(memory_space=pltpu.HBM),
                pl.BlockSpec(memory_space=pltpu.HBM),
                pl.BlockSpec(memory_space=pltpu.SMEM),
                pl.BlockSpec(memory_space=pltpu.HBM),
                pl.BlockSpec(memory_space=pltpu.HBM),
            ],
            out_specs=pl.BlockSpec(memory_space=pltpu.VMEM),
            scratch_shapes=[
                pltpu.VMEM((sep, depth), jnp.bfloat16),
                pltpu.VMEM((sep, depth), jnp.bfloat16),
                pltpu.VMEM((count, blocks, rows, LANES), f32),
                pltpu.VMEM((count, blocks, rows, LANES), f32),
                pltpu.VMEM((2, count, pieces, rows, LANES), f32),
                dma((2, count, 2)),
                dma((2, count, 3)),
                dma((count, steps, most_copies)),
                dma((count, steps, most_copies)),
                *[room(k) for k in range(steps)],
                *[landing(k) for k in range(steps)],
                pltpu.VMEM((depth, sep), panels.dtype),
                pltpu.VMEM(eigvals.shape, f32),
                pltpu.VMEM(separator_diag.shape, f32),
                pltpu.VMEM(tables.shape, tables.dtype),
                dma((4,)),
            ],
            compiler_params=pltpu.CompilerParams(
                collective_id=0, has_side_effects=True, vmem_limit_bytes=48 * 2**20
            ),
        )(panels, eigvals, counts, separator_diag, tables)
        return root * (1.0 / math.sqrt(subs))

    return jax.shard_map(
        local,
        mesh=mesh,
        in_specs=(P("sub", "mode", None), P("sub", "mode"), P("sub"), P("sub", None), P()),
        out_specs=P("sub", None),
        check_vma=False,
    )
```

```python
import functools
import math

import jax
import jax.numpy as jnp
from jax import lax
from jax.experimental import pallas as pl
from jax.experimental.pallas import tpu as pltpu
from jax.sharding import PartitionSpec as P

MESH = pl.DeviceIdType.MESH
NT = (((1,), (1,)), ((), ()))
LANES = 128
CORE = ("mode", 0)
SHARES = (24, 24)


def plan(subs, modes):
    if subs == 8 and modes == 4:
        x, y, near, far = ("mode", 1), ("sub", 0), ("sub", 1), ("sub", 2)
        return [
            [("halve", (x,)), ("halve", (y, near)), ("halve", (far,))],
            [("halve", (y,)), ("halve", (x, near)), ("halve", (far,))],
            [("halve", (near,)), ("halve", (x, y)), ("halve", (far,))],
        ], 2, SHARES
    sub_bits, mode_bits = subs.bit_length() - 1, modes.bit_length() - 1
    steps = [("halve", (("sub", b),)) for b in range(sub_bits)]
    steps += [("full", (("mode", b),)) for b in range(1, mode_bits)]
    return [steps] * 3, 1, None


def halved(phase):
    kind, dims = phase
    return dims if kind == "halve" else ()


def members(dims):
    return [
        (mask, tuple(d for i, d in enumerate(dims) if mask >> (len(dims) - 1 - i) & 1))
        for mask in range(1, 2 ** len(dims))
    ]


def bit_of(value, bit):
    return (value // 2**bit) % 2


def body(subs, modes, column_parts, pieces, shares, *refs):
    panels_hbm, eig_hbm, counts_ref, diag_hbm, tables_hbm, out_ref = refs[:6]
    panels_ref, eig_ref, diag_ref, tables_ref, load_sems = refs[-5:]
    wt, pt, to_core, from_core, fin, core_sems, last_sem, send_sems, recv_sems = refs[6:15]
    chunks, steps = len(column_parts), len(column_parts[0])
    spans = [pl.ds(sum(shares[:h]), share) for h, share in enumerate(shares)]
    order = [(q, h) for h in range(len(shares)) for q in range(chunks)]
    accs = refs[15 : 15 + steps]
    lands = refs[15 + steps : -5]
    loads = [
        pltpu.make_async_copy(source, kept, load_sems.at[i])
        for i, (source, kept) in enumerate(
            [
                (tables_hbm, tables_ref),
                (panels_hbm, panels_ref),
                (eig_hbm, eig_ref),
                (diag_hbm, diag_ref),
            ]
        )
    ]
    for load in loads:
        load.start()
    sub_me, mode_me = lax.axis_index("sub"), lax.axis_index("mode")
    core_me = mode_me % 2
    depth, sep = panels_ref.shape
    tall = sum(shares)
    blocks = subs * pieces
    place = {"sub": sub_me, "mode": mode_me}

    def partner(dims):
        there = dict(place)
        for axis, bit in dims:
            there[axis] = there[axis] + 2**bit * (1 - 2 * bit_of(place[axis], bit))
        return there["sub"], there["mode"]

    gather = [(CORE,)] if pieces == 1 else [(CORE,), (("mode", 1),), (CORE, ("mode", 1))]
    greeted = {tuple(sorted(dims)) for part in column_parts for _, group in part for _, dims in members(group)}
    greeted = sorted(greeted | set(gather))
    barrier = pltpu.get_barrier_semaphore()
    for dims in greeted:
        pl.semaphore_signal(barrier, inc=1, device_id=partner(dims), device_id_type=MESH)

    runs = sep // LANES
    lane = lax.broadcasted_iota(jnp.int32, (8, LANES), 1)
    run_of = lax.broadcasted_iota(jnp.int32, (8, LANES), 0)

    def look_up(line, at):
        found = jnp.zeros((8, LANES), line.dtype)
        for run in range(runs):
            table = jnp.broadcast_to(line[:, run * LANES : (run + 1) * LANES], (8, LANES))
            here = jnp.take_along_axis(table, at % LANES, axis=1)
            found = jnp.where(at // LANES == run, here, found)
        return found

    loads[0].wait()
    index = run_of * LANES + lane
    for level in reversed(range(subs.bit_length() - 1)):
        index = index + 97 * level % sep
        index = jnp.where(index >= sep, index - sep, index)
        at = (sub_me // 2**level) * 2**level + 2**level - 1
        index = look_up(tables_ref[pl.ds(at, 1), :], index)
    target = jnp.concatenate([index.T[:, run : run + 1] for run in range(runs)], axis=0)
    moved = jnp.where(
        target == lax.broadcasted_iota(jnp.int32, (sep, sep), 1), 1.0, 0.0
    ).astype(jnp.bfloat16)

    for load in loads[1:]:
        load.wait()
    live = lax.broadcasted_iota(jnp.int32, (1, depth), 1) + mode_me * depth < counts_ref[0]
    scale = jnp.where(live, 1.0, 0.0) / eig_ref[...]
    panels_t = lax.dot_general(moved, panels_ref[...], NT, preferred_element_type=jnp.float32)
    pt[...] = panels_t.astype(jnp.bfloat16)
    wt[...] = (panels_t * scale).astype(jnp.bfloat16)
    diag = look_up(diag_ref[...] * jnp.where(mode_me < 2, 1.0, 0.0), index)

    gathered = tall % 16 == 0
    off_diag = lax.broadcasted_iota(jnp.int32, (tall, LANES), 1) - lax.broadcasted_iota(
        jnp.int32, (tall, LANES), 0
    )

    def block_at(q, slot):
        sub, piece, bit_at = sub_me, bit_of(mode_me, 1) if pieces == 2 else 0, blocks.bit_length() - 2
        for phase in column_parts[q]:
            for axis, bit in halved(phase):
                if slot >> bit_at & 1:
                    if axis == "sub":
                        sub = sub + 2**bit * (1 - 2 * bit_of(sub_me, bit))
                    else:
                        piece = 1 - piece
                bit_at -= 1
        return sub * pieces + piece

    def slot_of(q, block):
        slot = 0
        for phase in column_parts[q]:
            for axis, bit in halved(phase):
                slot = slot * 2 + (block >> bit & 1) + bit_of(sub_me, bit) * (1 - 2 * (block >> bit & 1))
        return slot

    def form(q, slots):
        first = [pl.multiple_of((q * 2 + c) * LANES, LANES) for c in (1 - core_me, core_me)]
        columns = jnp.concatenate([pt[pl.ds(start, LANES), :] for start in first], axis=0)
        if gathered:
            starts = [pl.multiple_of(block_at(q, slot) * tall, 16) for slot in slots]
            left = jnp.concatenate([wt[pl.ds(start, tall), :] for start in starts], axis=0)
        else:
            starts = [block * tall for block in range(blocks)]
            slots = [slot_of(q, block) for block in range(blocks)]
            left = wt[...]
        product = lax.dot_general(left, columns, NT, preferred_element_type=jnp.float32)
        for i, slot in enumerate(slots):
            to_core[q, slot, :, :] = -product[i * tall : (i + 1) * tall, 0:LANES]
        mine = jnp.where(core_me == 0, diag[2 * q : 2 * q + 1], diag[2 * q + 1 : 2 * q + 2])
        for i, (slot, start) in enumerate(zip(slots, starts)):
            on_diag = jnp.where(off_diag == start - first[1], mine, 0.0)
            accs[0][q, slot, :, :] = on_diag - product[i * tall : (i + 1) * tall, LANES : 2 * LANES]

    bands = [(blocks // 2, blocks // 2), (0, blocks // 2)] if gathered else [(0, blocks)]

    def finish(ref, sem):
        pltpu.make_async_copy(ref, ref, sem).wait()

    def core_copy(q, band):
        at, n = bands[band]
        return pltpu.make_async_remote_copy(
            to_core.at[q, pl.ds(at, n)],
            from_core.at[q, pl.ds(at, n)],
            send_sems.at[steps],
            core_sems.at[q, band],
            partner((CORE,)),
            MESH,
        )

    sizes = []
    for part in column_parts:
        n, own = blocks, []
        for phase in part:
            n = n >> len(halved(phase))
            own.append(n)
        sizes.append(own)

    def exchange(q, h, k):
        kind, dims = column_parts[q][k]
        n = sizes[q][k]
        return [
            pltpu.make_async_remote_copy(
                accs[k].at[q, pl.ds(mask * n if kind == "halve" else 0, n), spans[h]],
                lands[k].at[q, pl.ds((mask - 1) * n, n), spans[h]],
                send_sems.at[k],
                recv_sems.at[q, h, k],
                partner(other),
                MESH,
            )
            for mask, other in members(dims)
        ]

    for band, (at, n) in enumerate(bands):
        for q in range(chunks):
            form(q, range(at, at + n))
            if band == 0 and q == 0:
                pl.semaphore_wait(barrier, len(greeted))
            core_copy(q, band).start()
    for band, (at, n) in enumerate(bands):
        for q in range(chunks):
            core_copy(q, band).wait_recv()
            accs[0][q, at : at + n] = accs[0][q, at : at + n] + from_core[q, at : at + n]
            if band == 0:
                for h in range(len(shares)):
                    for copy in exchange(q, h, 0):
                        copy.start()

    mine = core_me * pieces + (bit_of(mode_me, 1) if pieces == 2 else 0)

    def last_copies(q, h):
        spot = fin.at[pl.ds(mine, 1), q, spans[h]]
        return [
            pltpu.make_async_remote_copy(
                spot, spot, send_sems.at[steps + 1], last_sem, partner(dims), MESH
            )
            for dims in gather
        ]

    for k in range(steps):
        for q, h in order:
            n, span = sizes[q][k], spans[h]
            total = accs[k][q, 0:n, span]
            masks = members(column_parts[q][k][1])
            finish(lands[k].at[q, pl.ds(0, len(masks) * n), span], recv_sems.at[q, h, k])
            for mask, _ in masks:
                total = total + lands[k][q, (mask - 1) * n : mask * n, span]
            if k < steps - 1:
                accs[k + 1][q, 0:n, span] = total
                for copy in exchange(q, h, k + 1):
                    copy.start()
                continue
            fin[pl.ds(mine, 1), q, span] = total
            for copy in last_copies(q, h):
                copy.start()
    others = fin.at[pl.ds(0, len(gather))]
    finish(others, last_sem)
    for c in range(2):
        for q in range(chunks):
            at = (q * 2 + c) * LANES
            for piece in range(pieces):
                out_ref[piece * tall : (piece + 1) * tall, at : at + LANES] = fin[c * pieces + piece, q]
    for i, landing in enumerate([*lands, to_core, others]):
        finish(landing, send_sems.at[i])


def solution(mesh):
    subs, modes = mesh.shape["sub"], mesh.shape["mode"]
    column_parts, pieces, shares = plan(subs, modes)

    def local(panels, eigvals, counts, separator_diag, tables):
        sep, depth = panels.shape[2], panels.shape[1]
        own = sep // subs
        tall = own // pieces
        cut = shares or (tall,)
        count, steps, blocks = len(column_parts), len(column_parts[0]), subs * pieces
        f32 = jnp.float32

        def held(part, k):
            return blocks >> sum(len(halved(phase)) for phase in part[:k])

        def room(k):
            return pltpu.VMEM((count, max(held(part, k) for part in column_parts), tall, LANES), f32)

        def landing(k):
            most = max((2 ** len(part[k][1]) - 1) * held(part, k + 1) for part in column_parts)
            return pltpu.VMEM((count, most, tall, LANES), f32)

        dma = pltpu.SemaphoreType.DMA
        panels, eigvals, separator_diag, tables = [
            pltpu.with_memory_space_constraint(a, pltpu.HBM)
            for a in (panels[0], eigvals, separator_diag, tables)
        ]
        root = pl.pallas_call(
            functools.partial(body, subs, modes, column_parts, pieces, cut),
            out_shape=jax.ShapeDtypeStruct((own, sep), f32),
            in_specs=[
                pl.BlockSpec(memory_space=pltpu.HBM),
                pl.BlockSpec(memory_space=pltpu.HBM),
                pl.BlockSpec(memory_space=pltpu.SMEM),
                pl.BlockSpec(memory_space=pltpu.HBM),
                pl.BlockSpec(memory_space=pltpu.HBM),
            ],
            out_specs=pl.BlockSpec(memory_space=pltpu.VMEM),
            scratch_shapes=[
                pltpu.VMEM((sep, depth), jnp.bfloat16),
                pltpu.VMEM((sep, depth), jnp.bfloat16),
                pltpu.VMEM((count, blocks, tall, LANES), f32),
                pltpu.VMEM((count, blocks, tall, LANES), f32),
                pltpu.VMEM((2 * pieces, count, tall, LANES), f32),
                dma((count, 2)),
                dma(()),
                dma((steps + 2,)),
                dma((count, len(cut), steps)),
                *[room(k) for k in range(steps)],
                *[landing(k) for k in range(steps)],
                pltpu.VMEM((depth, sep), panels.dtype),
                pltpu.VMEM(eigvals.shape, f32),
                pltpu.VMEM(separator_diag.shape, f32),
                pltpu.VMEM(tables.shape, tables.dtype),
                dma((4,)),
            ],
            compiler_params=pltpu.CompilerParams(
                collective_id=0, has_side_effects=True, vmem_limit_bytes=48 * 2**20
            ),
        )(panels, eigvals, counts, separator_diag, tables)
        return root * (1.0 / math.sqrt(subs))

    return jax.shard_map(
        local,
        mesh=mesh,
        in_specs=(P("sub", "mode", None), P("sub", "mode"), P("sub"), P("sub", None), P()),
        out_specs=P("sub", None),
        check_vma=False,
    )
```

```python
import functools
import math

import jax
import jax.numpy as jnp
from jax import lax
from jax.experimental import pallas as pl
from jax.experimental.pallas import tpu as pltpu
from jax.sharding import PartitionSpec as P

MESH = pl.DeviceIdType.MESH
NT = (((1,), (1,)), ((), ()))
LANES = 128
CORE = ("mode", 0)
SHARES = (24, 24)


def plan(subs, modes):
    if subs == 8 and modes == 4:
        x, y, near, far = ("mode", 1), ("sub", 0), ("sub", 1), ("sub", 2)
        return [
            [("halve", (x,)), ("halve", (far,y)), ("halve", (near,))],
            [("halve", (y,)), ("halve", (near,x)), ("halve", (far,))],
            [("halve", (near,)), ("halve", (y,x)), ("halve", (far,))],
        ], 2, SHARES
    sub_bits, mode_bits = subs.bit_length() - 1, modes.bit_length() - 1
    steps = [("halve", (("sub", b),)) for b in range(sub_bits)]
    steps += [("full", (("mode", b),)) for b in range(1, mode_bits)]
    return [steps] * 3, 1, None


def halved(phase):
    kind, dims = phase
    return dims if kind == "halve" else ()


def members(dims):
    return [
        (mask, tuple(d for i, d in enumerate(dims) if mask >> (len(dims) - 1 - i) & 1))
        for mask in range(1, 2 ** len(dims))
    ]


def bit_of(value, bit):
    return (value // 2**bit) % 2


def body(subs, modes, column_parts, pieces, shares, *refs):
    panels_hbm, eig_hbm, counts_ref, diag_hbm, tables_hbm, out_ref = refs[:6]
    panels_ref, eig_ref, diag_ref, tables_ref, load_sems = refs[-5:]
    wt, pt, to_core, from_core, fin, core_sems, last_sem, send_sems, recv_sems = refs[6:15]
    chunks, steps = len(column_parts), len(column_parts[0])
    spans = [pl.ds(sum(shares[:h]), share) for h, share in enumerate(shares)]
    order = [(q, h) for h in range(len(shares)) for q in range(chunks)]
    accs = refs[15 : 15 + steps]
    lands = refs[15 + steps : -5]
    loads = [
        pltpu.make_async_copy(source, kept, load_sems.at[i])
        for i, (source, kept) in enumerate(
            [
                (tables_hbm, tables_ref),
                (panels_hbm, panels_ref),
                (eig_hbm, eig_ref),
                (diag_hbm, diag_ref),
            ]
        )
    ]
    for load in loads:
        load.start()
    sub_me, mode_me = lax.axis_index("sub"), lax.axis_index("mode")
    core_me = mode_me % 2
    depth, sep = panels_ref.shape
    tall = sum(shares)
    blocks = subs * pieces
    place = {"sub": sub_me, "mode": mode_me}

    def partner(dims):
        there = dict(place)
        for axis, bit in dims:
            there[axis] = there[axis] + 2**bit * (1 - 2 * bit_of(place[axis], bit))
        return there["sub"], there["mode"]

    gather = [(CORE,)] if pieces == 1 else [(CORE,), (("mode", 1),), (CORE, ("mode", 1))]
    greeted = {tuple(sorted(dims)) for part in column_parts for _, group in part for _, dims in members(group)}
    greeted = sorted(greeted | set(gather))
    barrier = pltpu.get_barrier_semaphore()
    for dims in greeted:
        pl.semaphore_signal(barrier, inc=1, device_id=partner(dims), device_id_type=MESH)

    runs = sep // LANES
    lane = lax.broadcasted_iota(jnp.int32, (8, LANES), 1)
    run_of = lax.broadcasted_iota(jnp.int32, (8, LANES), 0)

    def look_up(line, at):
        found = jnp.zeros((8, LANES), line.dtype)
        for run in range(runs):
            table = jnp.broadcast_to(line[:, run * LANES : (run + 1) * LANES], (8, LANES))
            here = jnp.take_along_axis(table, at % LANES, axis=1)
            found = jnp.where(at // LANES == run, here, found)
        return found

    loads[0].wait()
    index = run_of * LANES + lane
    for level in reversed(range(subs.bit_length() - 1)):
        index = index + 97 * level % sep
        index = jnp.where(index >= sep, index - sep, index)
        at = (sub_me // 2**level) * 2**level + 2**level - 1
        index = look_up(tables_ref[pl.ds(at, 1), :], index)
    target = jnp.concatenate([index.T[:, run : run + 1] for run in range(runs)], axis=0)
    moved = jnp.where(
        target == lax.broadcasted_iota(jnp.int32, (sep, sep), 1), 1.0, 0.0
    ).astype(jnp.bfloat16)

    for load in loads[1:]:
        load.wait()
    live = lax.broadcasted_iota(jnp.int32, (1, depth), 1) + mode_me * depth < counts_ref[0]
    scale = jnp.where(live, 1.0, 0.0) / eig_ref[...]
    panels_t = lax.dot_general(moved, panels_ref[...], NT, preferred_element_type=jnp.float32)
    pt[...] = panels_t.astype(jnp.bfloat16)
    wt[...] = (panels_t * scale).astype(jnp.bfloat16)
    diag = look_up(diag_ref[...] * jnp.where(mode_me < 2, 1.0, 0.0), index)

    gathered = tall % 16 == 0
    off_diag = lax.broadcasted_iota(jnp.int32, (tall, LANES), 1) - lax.broadcasted_iota(
        jnp.int32, (tall, LANES), 0
    )

    def block_at(q, slot):
        sub, piece, bit_at = sub_me, bit_of(mode_me, 1) if pieces == 2 else 0, blocks.bit_length() - 2
        for phase in column_parts[q]:
            for axis, bit in halved(phase):
                if slot >> bit_at & 1:
                    if axis == "sub":
                        sub = sub + 2**bit * (1 - 2 * bit_of(sub_me, bit))
                    else:
                        piece = 1 - piece
                bit_at -= 1
        return sub * pieces + piece

    def slot_of(q, block):
        slot = 0
        for phase in column_parts[q]:
            for axis, bit in halved(phase):
                slot = slot * 2 + (block >> bit & 1) + bit_of(sub_me, bit) * (1 - 2 * (block >> bit & 1))
        return slot

    def form(q, slots):
        first = [pl.multiple_of((q * 2 + c) * LANES, LANES) for c in (1 - core_me, core_me)]
        columns = jnp.concatenate([pt[pl.ds(start, LANES), :] for start in first], axis=0)
        if gathered:
            starts = [pl.multiple_of(block_at(q, slot) * tall, 16) for slot in slots]
            left = jnp.concatenate([wt[pl.ds(start, tall), :] for start in starts], axis=0)
        else:
            starts = [block * tall for block in range(blocks)]
            slots = [slot_of(q, block) for block in range(blocks)]
            left = wt[...]
        half = depth // 2
        product = sum(
            lax.dot_general(left[:, at : at + half], columns[:, at : at + half], NT, preferred_element_type=jnp.float32)
            for at in (0, half)
        )
        for i, slot in enumerate(slots):
            to_core[q, slot, :, :] = -product[i * tall : (i + 1) * tall, 0:LANES]
        mine = jnp.where(core_me == 0, diag[2 * q : 2 * q + 1], diag[2 * q + 1 : 2 * q + 2])
        for i, (slot, start) in enumerate(zip(slots, starts)):
            on_diag = jnp.where(off_diag == start - first[1], mine, 0.0)
            accs[0][q, slot, :, :] = on_diag - product[i * tall : (i + 1) * tall, LANES : 2 * LANES]

    bands = [(blocks // 2, blocks // 2), (0, blocks // 2)] if gathered else [(0, blocks)]

    def finish(ref, sem):
        pltpu.make_async_copy(ref, ref, sem).wait()

    def core_copy(q, band):
        at, n = bands[band]
        return pltpu.make_async_remote_copy(
            to_core.at[q, pl.ds(at, n)],
            from_core.at[q, pl.ds(at, n)],
            send_sems.at[steps],
            core_sems.at[q, band],
            partner((CORE,)),
            MESH,
        )

    sizes = []
    for part in column_parts:
        n, own = blocks, []
        for phase in part:
            n = n >> len(halved(phase))
            own.append(n)
        sizes.append(own)

    def exchange(q, h, k):
        kind, dims = column_parts[q][k]
        n = sizes[q][k]
        return [
            pltpu.make_async_remote_copy(
                accs[k].at[q, pl.ds(mask * n if kind == "halve" else 0, n), spans[h]],
                lands[k].at[q, pl.ds((mask - 1) * n, n), spans[h]],
                send_sems.at[k],
                recv_sems.at[q, h, k],
                partner(other),
                MESH,
            )
            for mask, other in members(dims)
        ]

    for band, (at, n) in enumerate(bands):
        for q in range(chunks):
            form(q, range(at, at + n))
            if band == 0 and q == 0:
                pl.semaphore_wait(barrier, len(greeted))
            core_copy(q, band).start()
    for band, (at, n) in enumerate(bands):
        for q in range(chunks):
            core_copy(q, band).wait_recv()
            accs[0][q, at : at + n] = accs[0][q, at : at + n] + from_core[q, at : at + n]
            if band == 0:
                for h in range(len(shares)):
                    for copy in exchange(q, h, 0):
                        copy.start()

    mine = core_me * pieces + (bit_of(mode_me, 1) if pieces == 2 else 0)

    def last_copies(q, h):
        spot = fin.at[pl.ds(mine, 1), q, spans[h]]
        return [
            pltpu.make_async_remote_copy(
                spot, spot, send_sems.at[steps + 1], last_sem, partner(dims), MESH
            )
            for dims in gather
        ]

    for k in range(steps):
        for q, h in order:
            n, span = sizes[q][k], spans[h]
            total = accs[k][q, 0:n, span]
            masks = members(column_parts[q][k][1])
            finish(lands[k].at[q, pl.ds(0, len(masks) * n), span], recv_sems.at[q, h, k])
            for mask, _ in masks:
                total = total + lands[k][q, (mask - 1) * n : mask * n, span]
            if k < steps - 1:
                accs[k + 1][q, 0:n, span] = total
                for copy in exchange(q, h, k + 1):
                    copy.start()
                continue
            fin[pl.ds(mine, 1), q, span] = total
            for copy in last_copies(q, h):
                copy.start()
    others = fin.at[pl.ds(0, len(gather))]
    finish(others, last_sem)
    for c in range(2):
        for q in range(chunks):
            at = (q * 2 + c) * LANES
            for piece in range(pieces):
                out_ref[piece * tall : (piece + 1) * tall, at : at + LANES] = fin[c * pieces + piece, q]
    for i, landing in enumerate([*lands, to_core, others]):
        finish(landing, send_sems.at[i])


def solution(mesh):
    subs, modes = mesh.shape["sub"], mesh.shape["mode"]
    column_parts, pieces, shares = plan(subs, modes)

    def local(panels, eigvals, counts, separator_diag, tables):
        sep, depth = panels.shape[2], panels.shape[1]
        own = sep // subs
        tall = own // pieces
        cut = shares or (tall,)
        count, steps, blocks = len(column_parts), len(column_parts[0]), subs * pieces
        f32 = jnp.float32

        def held(part, k):
            return blocks >> sum(len(halved(phase)) for phase in part[:k])

        def room(k):
            return pltpu.VMEM((count, max(held(part, k) for part in column_parts), tall, LANES), f32)

        def landing(k):
            most = max((2 ** len(part[k][1]) - 1) * held(part, k + 1) for part in column_parts)
            return pltpu.VMEM((count, most, tall, LANES), f32)

        dma = pltpu.SemaphoreType.DMA
        panels, eigvals, separator_diag, tables = [
            pltpu.with_memory_space_constraint(a, pltpu.HBM)
            for a in (panels[0], eigvals, separator_diag, tables)
        ]
        root = pl.pallas_call(
            functools.partial(body, subs, modes, column_parts, pieces, cut),
            out_shape=jax.ShapeDtypeStruct((own, sep), f32),
            in_specs=[
                pl.BlockSpec(memory_space=pltpu.HBM),
                pl.BlockSpec(memory_space=pltpu.HBM),
                pl.BlockSpec(memory_space=pltpu.SMEM),
                pl.BlockSpec(memory_space=pltpu.HBM),
                pl.BlockSpec(memory_space=pltpu.HBM),
            ],
            out_specs=pl.BlockSpec(memory_space=pltpu.VMEM),
            scratch_shapes=[
                pltpu.VMEM((sep, depth), jnp.bfloat16),
                pltpu.VMEM((sep, depth), jnp.bfloat16),
                pltpu.VMEM((count, blocks, tall, LANES), f32),
                pltpu.VMEM((count, blocks, tall, LANES), f32),
                pltpu.VMEM((2 * pieces, count, tall, LANES), f32),
                dma((count, 2)),
                dma(()),
                dma((steps + 2,)),
                dma((count, len(cut), steps)),
                *[room(k) for k in range(steps)],
                *[landing(k) for k in range(steps)],
                pltpu.VMEM((depth, sep), panels.dtype),
                pltpu.VMEM(eigvals.shape, f32),
                pltpu.VMEM(separator_diag.shape, f32),
                pltpu.VMEM(tables.shape, tables.dtype),
                dma((4,)),
            ],
            compiler_params=pltpu.CompilerParams(
                collective_id=0, has_side_effects=True, vmem_limit_bytes=48 * 2**20
            ),
        )(panels, eigvals, counts, separator_diag, tables)
        return root * (1.0 / math.sqrt(subs))

    return jax.shard_map(
        local,
        mesh=mesh,
        in_specs=(P("sub", "mode", None), P("sub", "mode"), P("sub"), P("sub", None), P()),
        out_specs=P("sub", None),
        check_vma=False,
    )
```

```python
import functools
import math

import jax
import jax.numpy as jnp
from jax import lax
from jax.experimental import pallas as pl
from jax.experimental.pallas import tpu as pltpu
from jax.sharding import PartitionSpec as P

MESH = pl.DeviceIdType.MESH
NT = (((1,), (1,)), ((), ()))
LANES = 128
CORE = ("mode", 0)
SHARES = (24, 24)


def plan(subs, modes):
    if subs == 8 and modes == 4:
        x, y, near, far = ("mode", 1), ("sub", 0), ("sub", 1), ("sub", 2)
        return [
            [("halve", (x,)), ("halve", (far,y)), ("halve", (near,))],
            [("halve", (y,)), ("halve", (near,x)), ("halve", (far,))],
            [("halve", (near,)), ("halve", (y,x)), ("halve", (far,))],
        ], 2, SHARES
    sub_bits, mode_bits = subs.bit_length() - 1, modes.bit_length() - 1
    steps = [("halve", (("sub", b),)) for b in range(sub_bits)]
    steps += [("full", (("mode", b),)) for b in range(1, mode_bits)]
    return [steps] * 3, 1, None


def halved(phase):
    kind, dims = phase
    return dims if kind == "halve" else ()


def members(dims):
    return [
        (mask, tuple(d for i, d in enumerate(dims) if mask >> (len(dims) - 1 - i) & 1))
        for mask in range(1, 2 ** len(dims))
    ]


def bit_of(value, bit):
    return (value // 2**bit) % 2


def body(subs, modes, column_parts, pieces, shares, *refs):
    panels_hbm, eig_hbm, counts_ref, diag_hbm, tables_hbm, out_ref = refs[:6]
    panels_ref, eig_ref, diag_ref, tables_ref, load_sems = refs[-5:]
    wt, pt, to_core, from_core, fin, core_sems, last_sem, send_sems, recv_sems = refs[6:15]
    chunks, steps = len(column_parts), len(column_parts[0])
    spans = [pl.ds(sum(shares[:h]), share) for h, share in enumerate(shares)]
    order = [(q, h) for h in range(len(shares)) for q in range(chunks)]
    accs = refs[15 : 15 + steps]
    lands = refs[15 + steps : -5]
    loads = [
        pltpu.make_async_copy(source, kept, load_sems.at[i])
        for i, (source, kept) in enumerate(
            [
                (tables_hbm, tables_ref),
                (panels_hbm, panels_ref),
                (eig_hbm, eig_ref),
                (diag_hbm, diag_ref),
            ]
        )
    ]
    for load in loads:
        load.start()
    sub_me, mode_me = lax.axis_index("sub"), lax.axis_index("mode")
    core_me = mode_me % 2
    depth, sep = panels_ref.shape
    tall = sum(shares)
    blocks = subs * pieces
    place = {"sub": sub_me, "mode": mode_me}

    def partner(dims):
        there = dict(place)
        for axis, bit in dims:
            there[axis] = there[axis] + 2**bit * (1 - 2 * bit_of(place[axis], bit))
        return there["sub"], there["mode"]

    gather = [(CORE,)] if pieces == 1 else [(CORE,), (("mode", 1),), (CORE, ("mode", 1))]
    greeted = {tuple(sorted(dims)) for part in column_parts for _, group in part for _, dims in members(group)}
    greeted = sorted(greeted | set(gather))
    barrier = pltpu.get_barrier_semaphore()
    for dims in greeted:
        pl.semaphore_signal(barrier, inc=1, device_id=partner(dims), device_id_type=MESH)

    runs = sep // LANES
    lane = lax.broadcasted_iota(jnp.int32, (8, LANES), 1)
    run_of = lax.broadcasted_iota(jnp.int32, (8, LANES), 0)

    def look_up(line, at):
        found = jnp.zeros((8, LANES), line.dtype)
        for run in range(runs):
            table = jnp.broadcast_to(line[:, run * LANES : (run + 1) * LANES], (8, LANES))
            here = jnp.take_along_axis(table, at % LANES, axis=1)
            found = jnp.where(at // LANES == run, here, found)
        return found

    loads[0].wait()
    index = run_of * LANES + lane
    for level in reversed(range(subs.bit_length() - 1)):
        index = index + 97 * level % sep
        index = jnp.where(index >= sep, index - sep, index)
        at = (sub_me // 2**level) * 2**level + 2**level - 1
        index = look_up(tables_ref[pl.ds(at, 1), :], index)
    target = jnp.concatenate([index.T[:, run : run + 1] for run in range(runs)], axis=0)
    moved = jnp.where(
        target == lax.broadcasted_iota(jnp.int32, (sep, sep), 1), 1.0, 0.0
    ).astype(jnp.bfloat16)

    for load in loads[1:]:
        load.wait()
    live = lax.broadcasted_iota(jnp.int32, (1, depth), 1) + mode_me * depth < counts_ref[0]
    scale = jnp.where(live, 1.0, 0.0) / eig_ref[...]
    panels_t = lax.dot_general(moved, panels_ref[...], NT, preferred_element_type=jnp.float32)
    pt[...] = panels_t.astype(jnp.bfloat16)
    wt[...] = (panels_t * scale).astype(jnp.bfloat16)
    diag = look_up(diag_ref[...] * jnp.where(mode_me < 2, 1.0, 0.0), index)

    gathered = tall % 16 == 0
    off_diag = lax.broadcasted_iota(jnp.int32, (tall, LANES), 1) - lax.broadcasted_iota(
        jnp.int32, (tall, LANES), 0
    )

    def block_at(q, slot):
        sub, piece, bit_at = sub_me, bit_of(mode_me, 1) if pieces == 2 else 0, blocks.bit_length() - 2
        for phase in column_parts[q]:
            for axis, bit in halved(phase):
                if slot >> bit_at & 1:
                    if axis == "sub":
                        sub = sub + 2**bit * (1 - 2 * bit_of(sub_me, bit))
                    else:
                        piece = 1 - piece
                bit_at -= 1
        return sub * pieces + piece

    def slot_of(q, block):
        slot = 0
        for phase in column_parts[q]:
            for axis, bit in halved(phase):
                slot = slot * 2 + (block >> bit & 1) + bit_of(sub_me, bit) * (1 - 2 * (block >> bit & 1))
        return slot

    def form(q, slots):
        first = [pl.multiple_of((q * 2 + c) * LANES, LANES) for c in (1 - core_me, core_me)]
        columns = jnp.concatenate([pt[pl.ds(start, LANES), :] for start in first], axis=0)
        if gathered:
            starts = [pl.multiple_of(block_at(q, slot) * tall, 16) for slot in slots]
            left = jnp.concatenate([wt[pl.ds(start, tall), :] for start in starts], axis=0)
        else:
            starts = [block * tall for block in range(blocks)]
            slots = [slot_of(q, block) for block in range(blocks)]
            left = wt[...]
        half = depth // 2
        product = sum(
            lax.dot_general(left[:, at : at + half], columns[:, at : at + half], NT, preferred_element_type=jnp.float32)
            for at in (0, half)
        )
        for i, slot in enumerate(slots):
            to_core[q, slot, :, :] = -product[i * tall : (i + 1) * tall, 0:LANES]
        mine = jnp.where(core_me == 0, diag[2 * q : 2 * q + 1], diag[2 * q + 1 : 2 * q + 2])
        for i, (slot, start) in enumerate(zip(slots, starts)):
            on_diag = jnp.where(off_diag == start - first[1], mine, 0.0)
            accs[0][q, slot, :, :] = on_diag - product[i * tall : (i + 1) * tall, LANES : 2 * LANES]

    bands = [(blocks // 2, blocks // 2), (0, blocks // 2)] if gathered else [(0, blocks)]

    def finish(ref, sem):
        pltpu.make_async_copy(ref, ref, sem).wait()

    whole = pl.ds(0, tall)
    pieces_out = [(q, 0, h, span) for h, span in enumerate(spans) for q in range(chunks)]
    pieces_out += [(q, band, 0, whole) for band in range(1, len(bands)) for q in range(chunks)]

    def core_copy(q, band, h, span):
        at, n = bands[band]
        return pltpu.make_async_remote_copy(
            to_core.at[q, pl.ds(at, n), span],
            from_core.at[q, pl.ds(at, n), span],
            send_sems.at[steps],
            core_sems.at[q, band * len(spans) + h],
            partner((CORE,)),
            MESH,
        )

    sizes = []
    for part in column_parts:
        n, own = blocks, []
        for phase in part:
            n = n >> len(halved(phase))
            own.append(n)
        sizes.append(own)

    def exchange(q, h, k):
        kind, dims = column_parts[q][k]
        n = sizes[q][k]
        return [
            pltpu.make_async_remote_copy(
                accs[k].at[q, pl.ds(mask * n if kind == "halve" else 0, n), spans[h]],
                lands[k].at[q, pl.ds((mask - 1) * n, n), spans[h]],
                send_sems.at[k],
                recv_sems.at[q, h, k],
                partner(other),
                MESH,
            )
            for mask, other in members(dims)
        ]

    for band, (at, n) in enumerate(bands):
        for q in range(chunks):
            form(q, range(at, at + n))
        if band == 0:
            pl.semaphore_wait(barrier, len(greeted))
        for piece in pieces_out:
            if piece[1] == band:
                core_copy(*piece).start()
    for q, band, h, span in pieces_out:
        at, n = bands[band]
        core_copy(q, band, h, span).wait_recv()
        accs[0][q, at : at + n, span] = accs[0][q, at : at + n, span] + from_core[q, at : at + n, span]
        if band == 0:
            for copy in exchange(q, h, 0):
                copy.start()

    mine = core_me * pieces + (bit_of(mode_me, 1) if pieces == 2 else 0)

    def last_copies(q, h):
        spot = fin.at[pl.ds(mine, 1), q, spans[h]]
        return [
            pltpu.make_async_remote_copy(
                spot, spot, send_sems.at[steps + 1], last_sem, partner(dims), MESH
            )
            for dims in gather
        ]

    for k in range(steps):
        for q, h in order:
            n, span = sizes[q][k], spans[h]
            total = accs[k][q, 0:n, span]
            masks = members(column_parts[q][k][1])
            finish(lands[k].at[q, pl.ds(0, len(masks) * n), span], recv_sems.at[q, h, k])
            for mask, _ in masks:
                total = total + lands[k][q, (mask - 1) * n : mask * n, span]
            if k < steps - 1:
                accs[k + 1][q, 0:n, span] = total
                for copy in exchange(q, h, k + 1):
                    copy.start()
                continue
            fin[pl.ds(mine, 1), q, span] = total
            for copy in last_copies(q, h):
                copy.start()
    others = fin.at[pl.ds(0, len(gather))]
    finish(others, last_sem)
    for c in range(2):
        for q in range(chunks):
            at = (q * 2 + c) * LANES
            for piece in range(pieces):
                out_ref[piece * tall : (piece + 1) * tall, at : at + LANES] = fin[c * pieces + piece, q]
    for i, landing in enumerate([*lands, to_core, others]):
        finish(landing, send_sems.at[i])


def solution(mesh):
    subs, modes = mesh.shape["sub"], mesh.shape["mode"]
    column_parts, pieces, shares = plan(subs, modes)

    def local(panels, eigvals, counts, separator_diag, tables):
        sep, depth = panels.shape[2], panels.shape[1]
        own = sep // subs
        tall = own // pieces
        cut = shares or (tall,)
        count, steps, blocks = len(column_parts), len(column_parts[0]), subs * pieces
        f32 = jnp.float32

        def held(part, k):
            return blocks >> sum(len(halved(phase)) for phase in part[:k])

        def room(k):
            return pltpu.VMEM((count, max(held(part, k) for part in column_parts), tall, LANES), f32)

        def landing(k):
            most = max((2 ** len(part[k][1]) - 1) * held(part, k + 1) for part in column_parts)
            return pltpu.VMEM((count, most, tall, LANES), f32)

        dma = pltpu.SemaphoreType.DMA
        panels, eigvals, separator_diag, tables = [
            pltpu.with_memory_space_constraint(a, pltpu.HBM)
            for a in (panels[0], eigvals, separator_diag, tables)
        ]
        root = pl.pallas_call(
            functools.partial(body, subs, modes, column_parts, pieces, cut),
            out_shape=jax.ShapeDtypeStruct((own, sep), f32),
            in_specs=[
                pl.BlockSpec(memory_space=pltpu.HBM),
                pl.BlockSpec(memory_space=pltpu.HBM),
                pl.BlockSpec(memory_space=pltpu.SMEM),
                pl.BlockSpec(memory_space=pltpu.HBM),
                pl.BlockSpec(memory_space=pltpu.HBM),
            ],
            out_specs=pl.BlockSpec(memory_space=pltpu.VMEM),
            scratch_shapes=[
                pltpu.VMEM((sep, depth), jnp.bfloat16),
                pltpu.VMEM((sep, depth), jnp.bfloat16),
                pltpu.VMEM((count, blocks, tall, LANES), f32),
                pltpu.VMEM((count, blocks, tall, LANES), f32),
                pltpu.VMEM((2 * pieces, count, tall, LANES), f32),
                dma((count, len(cut) + 1)),
                dma(()),
                dma((steps + 2,)),
                dma((count, len(cut), steps)),
                *[room(k) for k in range(steps)],
                *[landing(k) for k in range(steps)],
                pltpu.VMEM((depth, sep), panels.dtype),
                pltpu.VMEM(eigvals.shape, f32),
                pltpu.VMEM(separator_diag.shape, f32),
                pltpu.VMEM(tables.shape, tables.dtype),
                dma((4,)),
            ],
            compiler_params=pltpu.CompilerParams(
                collective_id=0, has_side_effects=True, vmem_limit_bytes=48 * 2**20
            ),
        )(panels, eigvals, counts, separator_diag, tables)
        return root * (1.0 / math.sqrt(subs))

    return jax.shard_map(
        local,
        mesh=mesh,
        in_specs=(P("sub", "mode", None), P("sub", "mode"), P("sub"), P("sub", None), P()),
        out_specs=P("sub", None),
        check_vma=False,
    )
```

```python
import functools
import math

import jax
import jax.numpy as jnp
from jax import lax
from jax.experimental import pallas as pl
from jax.experimental.pallas import tpu as pltpu
from jax.sharding import PartitionSpec as P

MESH = pl.DeviceIdType.MESH
NT = (((1,), (1,)), ((), ()))
LANES = 128
CORE = ("mode", 0)
SHARES = (16, 16, 16)


def plan(subs, modes):
    if subs == 8 and modes == 4:
        x, y, near, far = ("mode", 1), ("sub", 0), ("sub", 1), ("sub", 2)
        return [
            [("halve", (x,)), ("halve", (far, y)), ("dup", (near, x))],
            [("halve", (y,)), ("halve", (near, x)), ("dup", (far, x))],
            [("halve", (near,)), ("halve", (y, x)), ("dup", (far, x))],
        ], 2, SHARES
    sub_bits, mode_bits = subs.bit_length() - 1, modes.bit_length() - 1
    steps = [("halve", (("sub", b),)) for b in range(sub_bits)]
    steps += [("full", (("mode", b),)) for b in range(1, mode_bits)]
    return [steps] * 3, 1, None


def halved(phase):
    kind, dims = phase
    return {"halve": dims, "full": (), "dup": dims[:1]}[kind]


def members(dims):
    return [
        (mask, tuple(d for i, d in enumerate(dims) if mask >> (len(dims) - 1 - i) & 1))
        for mask in range(1, 2 ** len(dims))
    ]


def bit_of(value, bit):
    return (value // 2**bit) % 2


def body(subs, modes, column_parts, pieces, shares, *refs):
    panels_hbm, eig_hbm, counts_ref, diag_hbm, tables_hbm, out_ref = refs[:6]
    panels_ref, eig_ref, diag_ref, tables_ref, load_sems = refs[-5:]
    wt, pt, to_core, from_core, fin, core_sems, last_sem, send_sems, recv_sems = refs[6:15]
    chunks, steps = len(column_parts), len(column_parts[0])
    spans = [pl.ds(sum(shares[:h]), share) for h, share in enumerate(shares)]
    order = [(q, h) for h in range(len(shares)) for q in range(chunks)]
    accs = refs[15 : 15 + steps]
    lands = refs[15 + steps : -5]
    loads = [
        pltpu.make_async_copy(source, kept, load_sems.at[i])
        for i, (source, kept) in enumerate(
            [
                (tables_hbm, tables_ref),
                (panels_hbm, panels_ref),
                (eig_hbm, eig_ref),
                (diag_hbm, diag_ref),
            ]
        )
    ]
    for load in loads:
        load.start()
    sub_me, mode_me = lax.axis_index("sub"), lax.axis_index("mode")
    core_me = mode_me % 2
    depth, sep = panels_ref.shape
    tall = sum(shares)
    blocks = subs * pieces
    place = {"sub": sub_me, "mode": mode_me}

    def partner(dims):
        there = dict(place)
        for axis, bit in dims:
            there[axis] = there[axis] + 2**bit * (1 - 2 * bit_of(place[axis], bit))
        return there["sub"], there["mode"]

    gather = [(CORE,)]
    greeted = {tuple(sorted(dims)) for part in column_parts for _, group in part for _, dims in members(group)}
    greeted = sorted(greeted | set(gather))
    barrier = pltpu.get_barrier_semaphore()
    for dims in greeted:
        pl.semaphore_signal(barrier, inc=1, device_id=partner(dims), device_id_type=MESH)

    runs = sep // LANES
    lane = lax.broadcasted_iota(jnp.int32, (8, LANES), 1)
    run_of = lax.broadcasted_iota(jnp.int32, (8, LANES), 0)

    def look_up(line, at):
        found = jnp.zeros((8, LANES), line.dtype)
        for run in range(runs):
            table = jnp.broadcast_to(line[:, run * LANES : (run + 1) * LANES], (8, LANES))
            here = jnp.take_along_axis(table, at % LANES, axis=1)
            found = jnp.where(at // LANES == run, here, found)
        return found

    loads[0].wait()
    index = run_of * LANES + lane
    for level in reversed(range(subs.bit_length() - 1)):
        index = index + 97 * level % sep
        index = jnp.where(index >= sep, index - sep, index)
        at = (sub_me // 2**level) * 2**level + 2**level - 1
        index = look_up(tables_ref[pl.ds(at, 1), :], index)
    target = jnp.concatenate([index.T[:, run : run + 1] for run in range(runs)], axis=0)
    moved = jnp.where(
        target == lax.broadcasted_iota(jnp.int32, (sep, sep), 1), 1.0, 0.0
    ).astype(jnp.bfloat16)

    for load in loads[1:]:
        load.wait()
    live = lax.broadcasted_iota(jnp.int32, (1, depth), 1) + mode_me * depth < counts_ref[0]
    scale = jnp.where(live, 1.0, 0.0) / eig_ref[...]
    panels_t = lax.dot_general(moved, panels_ref[...], NT, preferred_element_type=jnp.float32)
    pt[...] = panels_t.astype(jnp.bfloat16)
    wt[...] = (panels_t * scale).astype(jnp.bfloat16)
    diag = look_up(diag_ref[...] * jnp.where(mode_me < 2, 1.0, 0.0), index)

    gathered = tall % 16 == 0
    off_diag = lax.broadcasted_iota(jnp.int32, (tall, LANES), 1) - lax.broadcasted_iota(
        jnp.int32, (tall, LANES), 0
    )

    def block_at(q, slot):
        sub, piece, bit_at = sub_me, bit_of(mode_me, 1) if pieces == 2 else 0, blocks.bit_length() - 2
        for phase in column_parts[q]:
            for axis, bit in halved(phase):
                if slot >> bit_at & 1:
                    if axis == "sub":
                        sub = sub + 2**bit * (1 - 2 * bit_of(sub_me, bit))
                    else:
                        piece = 1 - piece
                bit_at -= 1
        return sub * pieces + piece

    def slot_of(q, block):
        slot = 0
        for phase in column_parts[q]:
            for axis, bit in halved(phase):
                slot = slot * 2 + (block >> bit & 1) + bit_of(sub_me, bit) * (1 - 2 * (block >> bit & 1))
        return slot

    def form(q, slots):
        first = [pl.multiple_of((q * 2 + c) * LANES, LANES) for c in (1 - core_me, core_me)]
        columns = jnp.concatenate([pt[pl.ds(start, LANES), :] for start in first], axis=0)
        if gathered:
            starts = [pl.multiple_of(block_at(q, slot) * tall, 16) for slot in slots]
            left = jnp.concatenate([wt[pl.ds(start, tall), :] for start in starts], axis=0)
        else:
            starts = [block * tall for block in range(blocks)]
            slots = [slot_of(q, block) for block in range(blocks)]
            left = wt[...]
        half = depth // 2
        product = sum(
            lax.dot_general(left[:, at : at + half], columns[:, at : at + half], NT, preferred_element_type=jnp.float32)
            for at in (0, half)
        )
        for i, slot in enumerate(slots):
            to_core[q, slot, :, :] = -product[i * tall : (i + 1) * tall, 0:LANES]
        return lambda: keep(q, slots, starts, first, product)

    def keep(q, slots, starts, first, product):
        mine = jnp.where(core_me == 0, diag[2 * q : 2 * q + 1], diag[2 * q + 1 : 2 * q + 2])
        for i, (slot, start) in enumerate(zip(slots, starts)):
            on_diag = jnp.where(off_diag == start - first[1], mine, 0.0)
            accs[0][q, slot, :, :] = on_diag - product[i * tall : (i + 1) * tall, LANES : 2 * LANES]

    bands = [(blocks // 2, blocks // 2), (0, blocks // 2)] if gathered else [(0, blocks)]

    def finish(ref, sem):
        pltpu.make_async_copy(ref, ref, sem).wait()

    whole = pl.ds(0, tall)
    pieces_out = [(q, 0, h, span) for h, span in enumerate(spans) for q in range(chunks)]
    pieces_out += [(q, band, 0, whole) for band in range(1, len(bands)) for q in range(chunks)]

    def core_copy(q, band, h, span):
        at, n = bands[band]
        return pltpu.make_async_remote_copy(
            to_core.at[q, pl.ds(at, n), span],
            from_core.at[q, pl.ds(at, n), span],
            send_sems.at[steps],
            core_sems.at[q, band * len(spans) + h],
            partner((CORE,)),
            MESH,
        )

    sizes = []
    for part in column_parts:
        n, own = blocks, []
        for phase in part:
            n = n >> len(halved(phase))
            own.append(n)
        sizes.append(own)

    def exchange(q, h, k):
        kind, dims = column_parts[q][k]
        n = sizes[q][k]
        return [
            pltpu.make_async_remote_copy(
                accs[k].at[q, pl.ds({"halve": mask, "full": 0, "dup": mask // 2}[kind] * n, n), spans[h]],
                lands[k].at[q, pl.ds((mask - 1) * n, n), spans[h]],
                send_sems.at[k],
                recv_sems.at[q, h, k],
                partner(other),
                MESH,
            )
            for mask, other in members(dims)
        ]

    for band, (at, n) in enumerate(bands):
        rest = [form(q, range(at, at + n)) for q in range(chunks)]
        if band == 0:
            pl.semaphore_wait(barrier, len(greeted))
        for piece in pieces_out:
            if piece[1] == band:
                core_copy(*piece).start()
        for store in rest:
            store()
    for q, band, h, span in pieces_out:
        at, n = bands[band]
        core_copy(q, band, h, span).wait_recv()
        accs[0][q, at : at + n, span] = accs[0][q, at : at + n, span] + from_core[q, at : at + n, span]
        if band == 0:
            for copy in exchange(q, h, 0):
                copy.start()

    mine = core_me * pieces + (bit_of(mode_me, 1) if pieces == 2 else 0)
    there = core_me * pieces + pieces - 1 - (mine - core_me * pieces)

    def last_copies(q, h):
        spot = fin.at[pl.ds(core_me * pieces, pieces), q, spans[h]]
        return [
            pltpu.make_async_remote_copy(
                spot, spot, send_sems.at[steps + 1], last_sem, partner(dims), MESH
            )
            for dims in gather
        ]

    for k in range(steps):
        for q, h in order:
            n, span = sizes[q][k], spans[h]
            total = accs[k][q, 0:n, span]
            masks = members(column_parts[q][k][1])
            finish(lands[k].at[q, pl.ds(0, len(masks) * n), span], recv_sems.at[q, h, k])
            if column_parts[q][k][0] == "dup":
                land = lands[k]
                fin[pl.ds(mine, 1), q, span] = total + land[q, 1:2, span]
                fin[pl.ds(there, 1), q, span] = land[q, 0:1, span] + land[q, 2:3, span]
                for copy in last_copies(q, h):
                    copy.start()
                continue
            for mask, _ in masks:
                total = total + lands[k][q, (mask - 1) * n : mask * n, span]
            if k < steps - 1:
                accs[k + 1][q, 0:n, span] = total
                for copy in exchange(q, h, k + 1):
                    copy.start()
                continue
            fin[pl.ds(mine, 1), q, span] = total
            for copy in last_copies(q, h):
                copy.start()
    others = fin.at[pl.ds(0, pieces)]
    finish(others, last_sem)
    for c in range(2):
        for q in range(chunks):
            at = (q * 2 + c) * LANES
            for piece in range(pieces):
                out_ref[piece * tall : (piece + 1) * tall, at : at + LANES] = fin[c * pieces + piece, q]
    for i, landing in enumerate([*lands, to_core, others]):
        finish(landing, send_sems.at[i])


def solution(mesh):
    subs, modes = mesh.shape["sub"], mesh.shape["mode"]
    column_parts, pieces, shares = plan(subs, modes)

    def local(panels, eigvals, counts, separator_diag, tables):
        sep, depth = panels.shape[2], panels.shape[1]
        own = sep // subs
        tall = own // pieces
        cut = shares or (tall,)
        count, steps, blocks = len(column_parts), len(column_parts[0]), subs * pieces
        f32 = jnp.float32

        def held(part, k):
            return blocks >> sum(len(halved(phase)) for phase in part[:k])

        def room(k):
            return pltpu.VMEM((count, max(held(part, k) for part in column_parts), tall, LANES), f32)

        def landing(k):
            most = max((2 ** len(part[k][1]) - 1) * held(part, k + 1) for part in column_parts)
            return pltpu.VMEM((count, most, tall, LANES), f32)

        dma = pltpu.SemaphoreType.DMA
        panels, eigvals, separator_diag, tables = [
            pltpu.with_memory_space_constraint(a, pltpu.HBM)
            for a in (panels[0], eigvals, separator_diag, tables)
        ]
        root = pl.pallas_call(
            functools.partial(body, subs, modes, column_parts, pieces, cut),
            out_shape=jax.ShapeDtypeStruct((own, sep), f32),
            in_specs=[
                pl.BlockSpec(memory_space=pltpu.HBM),
                pl.BlockSpec(memory_space=pltpu.HBM),
                pl.BlockSpec(memory_space=pltpu.SMEM),
                pl.BlockSpec(memory_space=pltpu.HBM),
                pl.BlockSpec(memory_space=pltpu.HBM),
            ],
            out_specs=pl.BlockSpec(memory_space=pltpu.VMEM),
            scratch_shapes=[
                pltpu.VMEM((sep, depth), jnp.bfloat16),
                pltpu.VMEM((sep, depth), jnp.bfloat16),
                pltpu.VMEM((count, blocks, tall, LANES), f32),
                pltpu.VMEM((count, blocks, tall, LANES), f32),
                pltpu.VMEM((2 * pieces, count, tall, LANES), f32),
                dma((count, len(cut) + 1)),
                dma(()),
                dma((steps + 2,)),
                dma((count, len(cut), steps)),
                *[room(k) for k in range(steps)],
                *[landing(k) for k in range(steps)],
                pltpu.VMEM((depth, sep), panels.dtype),
                pltpu.VMEM(eigvals.shape, f32),
                pltpu.VMEM(separator_diag.shape, f32),
                pltpu.VMEM(tables.shape, tables.dtype),
                dma((4,)),
            ],
            compiler_params=pltpu.CompilerParams(
                collective_id=0, has_side_effects=True, vmem_limit_bytes=48 * 2**20
            ),
        )(panels, eigvals, counts, separator_diag, tables)
        return root * (1.0 / math.sqrt(subs))

    return jax.shard_map(
        local,
        mesh=mesh,
        in_specs=(P("sub", "mode", None), P("sub", "mode"), P("sub"), P("sub", None), P()),
        out_specs=P("sub", None),
        check_vma=False,
    )
```
